32 devices in a mesh: scen: 2 (over x), bus: 16 (over z, y, core).
Axes of the slice: x: 2, y: 2, z: 4, core: 2. Of those that a mesh axis runs over, the one named last changes fastest.
Arguments:
- injections: bfloat16 [256, 4096], P(('scen', 'bus')), may hold values from -6 to 6
- tile_values: bfloat16 [1024, 128, 128], P('bus', 'scen'), may hold values from -0.109375 to 0.109375
- tile_line: int32 [1024], P('bus'), may hold values from 0 to 47, as said below
- tile_bus: int32 [1024], P('bus'), may hold values from 0 to 1
- flow_pred: bfloat16 [256, 6144], P('scen', 'bus'), may hold values from -6 to 6
- line_limit: int32 [6144], P('bus'), may hold values from 50 to 199
Outputs:
- grad_injections: bfloat16 [256, 4096], P(('scen', 'bus'))
- flows: float32 [256, 6144], P('scen', 'bus')
The draws below stay inside these ranges and needn't reach their ends.
Inputs may be any that keep to these rules, and one draw needn't show every extreme that they name: `tile_line`: tile t is held by bus index t // 64; line block b is owned by bus index b // 3. Of the 64 tiles of one bus index at most 6 have line blocks of one owner, and in every draw some owner gets exactly 6 tiles from every bus index. A pair of line block and bus block may occur in several tiles; their values add.
All inputs are finite; a program needn't handle non-finite values.
Results may differ from the reference program's by a relative error of at most 0.0039.
Values may be sent and summed in bfloat16 or wider, within the bound.
A program may use at most 64 MiB of HBM per device.

```python
import jax
import jax.numpy as jnp
from jax import lax

TILE = 128
BB_DEV = 2
LB_DEV = 3
TILES_DEV = 64
CAP = 6
SCEN = 256
NBUS = 4096
NLINE = 6144
NTILE = 1024
N_BUS = 16


def plan_source(source_key, source, hot_owner, base_offset):
    key_scores, key_shuffle = jax.random.split(source_key, 2)
    slot_total = N_BUS * CAP
    scores = jax.random.permutation(key_scores, slot_total).astype(jnp.int32)
    positions = jnp.arange(slot_total, dtype=jnp.int32)
    peer_index = positions // CAP
    copy_index = positions % CAP
    scores = jnp.where(peer_index == hot_owner, scores + 2 * slot_total, scores)
    forced = ((peer_index == 0) | (peer_index == N_BUS - 1)) & (copy_index == 0) & (peer_index != hot_owner)
    scores = jnp.where(forced, scores - 2 * slot_total, scores)
    ordering = jnp.argsort(scores)
    chosen = peer_index[ordering[:TILES_DEV - CAP]]
    destination = jnp.concatenate([jnp.full((CAP,), hot_owner, jnp.int32), chosen.astype(jnp.int32)])
    owner_hits = (destination[:, None] == jnp.arange(N_BUS, dtype=jnp.int32)[None, :]).astype(jnp.int32)
    rank_within = jnp.sum(jnp.cumsum(owner_hits, axis=0) * owner_hits, axis=1) - 1
    offset_here = (source + base_offset) % LB_DEV
    local_block = (rank_within + offset_here) % LB_DEV
    line_blocks = destination * LB_DEV + local_block
    shuffle = jax.random.permutation(key_shuffle, TILES_DEV)
    return line_blocks[shuffle]


def draw_tile_line(key, part):
    key_hot, key_base, key_rest = jax.random.split(jax.random.fold_in(key, 11), 3)
    hot_owner = jax.random.randint(key_hot, (), 0, N_BUS).astype(jnp.int32)
    base_offset = jax.random.randint(key_base, (), 0, LB_DEV).astype(jnp.int32)
    source_keys = jax.random.split(key_rest, N_BUS)
    sources = jnp.arange(N_BUS, dtype=jnp.int32)
    planned = jax.vmap(plan_source, in_axes=(0, 0, None, None))(source_keys, sources, hot_owner, base_offset)
    return planned.reshape(N_BUS * TILES_DEV).astype(jnp.int32)


def place_ends(array, rng, least, largest):
    longest = array.shape.index(max(array.shape))
    spots = []
    for shift in (0, 1):
        where = [jax.random.randint(jax.random.fold_in(rng, axis), (), 0, length) for axis, length in enumerate(array.shape)]
        where[longest] = (where[longest] + shift) % array.shape[longest]
        spots.append(tuple(where))
    return array.at[spots[0]].set(least).at[spots[1]].set(largest)


def block_levels(own_key, extent, pieces, smallest, largest):
    def one(dim, shards_of):
        draws = jax.random.uniform(jax.random.fold_in(jax.random.fold_in(own_key, 6), dim), (shards_of,), jnp.float32, smallest / len(pieces), largest / len(pieces))
        return jnp.repeat(jnp.exp(draws), extent[dim] // shards_of).reshape((-1,) + (1,) * (len(extent) - dim - 1))

    loudness = one(*pieces[0])
    for cut in pieces[1:]:
        loudness = loudness * one(*cut)
    return loudness


def bell_draw(rng, dims, scale, bound, shards=(), kind=jnp.bfloat16):
    entries = scale * jax.random.normal(rng, dims, jnp.float32)
    if shards:
        entries = entries * block_levels(rng, dims, shards, -0.22, 0.18)
    return jnp.clip(entries, -bound, bound).astype(kind)


def setup_inputs(seed: int = 0) -> dict:
    arg_keys = jax.random.split(jax.random.key(seed), 7)
    return {
        "injections": bell_draw(arg_keys[0], (SCEN, NBUS), 1.0, 6.0, ((0, 32),)),
        "tile_values": bell_draw(arg_keys[1], (NTILE, TILE, TILE), (TILE * TILES_DEV // LB_DEV) ** -0.5, 0.109375, ((0, 16), (1, 2))),
        "tile_line": draw_tile_line(jax.random.fold_in(arg_keys[6], 71), 0),
        "tile_bus": place_ends(jax.random.randint(arg_keys[3], (NTILE,), 0, BB_DEV), jax.random.fold_in(arg_keys[3], 1), 0, BB_DEV - 1).astype(jnp.int32),
        "flow_pred": bell_draw(arg_keys[4], (SCEN, NLINE), 1.0, 6.0, ((0, 2), (1, 16))),
        "line_limit": place_ends(jax.random.randint(arg_keys[5], (NLINE,), 50, 200), jax.random.fold_in(arg_keys[5], 1), 50, 199).astype(jnp.int32),
    }


def reference(injections, tile_values, tile_line, tile_bus, flow_pred, line_limit):
    scen_count = injections.shape[0]
    inj_blocks = injections.astype(jnp.float32).reshape(scen_count, N_BUS * BB_DEV, TILE)
    tile_float = tile_values.astype(jnp.float32).reshape(N_BUS, TILES_DEV, TILE, TILE)
    bus_global = (jnp.arange(N_BUS * TILES_DEV, dtype=jnp.int32) // TILES_DEV) * BB_DEV + tile_bus.astype(jnp.int32)
    lines_grouped = tile_line.astype(jnp.int32).reshape(N_BUS, TILES_DEV)
    buses_grouped = bus_global.reshape(N_BUS, TILES_DEV)

    def forward_step(flow_acc, inputs):
        tile_group, line_group, bus_group = inputs
        selected = jnp.take(inj_blocks, bus_group, axis=1)
        partial_flows = jnp.einsum("stb,tlb->stl", selected, tile_group, precision=lax.Precision.HIGHEST)
        return flow_acc.at[:, line_group, :].add(partial_flows), None

    flow_zero = jnp.zeros((scen_count, N_BUS * LB_DEV, TILE), jnp.float32)
    flow_acc, unused_a = lax.scan(forward_step, flow_zero, (tile_float, lines_grouped, buses_grouped))
    flows = flow_acc.reshape(scen_count, N_BUS * LB_DEV * TILE)
    line_cap = line_limit.astype(jnp.float32) * 0.01
    residual = flows - flow_pred.astype(jnp.float32)
    grad_flow = (residual + jax.nn.sigmoid(4.0 * (flows - line_cap)) - jax.nn.sigmoid(4.0 * (-flows - line_cap))).astype(jnp.bfloat16)
    grad_blocks = grad_flow.astype(jnp.float32).reshape(scen_count, N_BUS * LB_DEV, TILE)

    def backward_step(grad_acc, inputs):
        tile_group, line_group, bus_group = inputs
        selected = jnp.take(grad_blocks, line_group, axis=1)
        contrib = jnp.einsum("stl,tlb->stb", selected, tile_group, precision=lax.Precision.HIGHEST)
        return grad_acc.at[:, bus_group, :].add(contrib), None

    grad_zero = jnp.zeros((scen_count, N_BUS * BB_DEV, TILE), jnp.float32)
    grad_acc, unused_b = lax.scan(backward_step, grad_zero, (tile_float, lines_grouped, buses_grouped))
    grad_injections = grad_acc.reshape(scen_count, N_BUS * BB_DEV * TILE).astype(jnp.bfloat16)
    return grad_injections, flows
```

```python
import jax
import jax.numpy as jnp
from jax import lax
from jax.experimental import pallas as pl
from jax.experimental.pallas import tpu as pltpu
from jax.sharding import PartitionSpec as P

MESH_ID = pl.DeviceIdType.MESH
F32 = jnp.float32
BF16 = jnp.bfloat16


def kernel(inj_ref, tiles_ref, line_ref, busid_ref, pred_ref, lim_ref, gout_ref, fout_ref,
           table_v, table_s, inj_buf, inj_t, dense, dense_t,
           csend, crecv, ysend, yrecv, acc, zsend, zrecv,
           pred_recv, pred_t, fx_send, fx_recv, fx_own,
           ag, gx_send, gx_own, gx_recv, gsend, grecv,
           table_sem, inj_ss, inj_rs, pred_sem, c_ss, c_rs, y_ss, y_rs, z_ss, z_rs,
           fx_sem, az_ss, az_rs, ay_ss, ay_rs, ac_ss, ac_rs, gx_sem, out_ss, out_rs):
    s = lax.axis_index("scen")
    b = lax.axis_index("bus")
    c = b % 2
    y = (b // 2) % 2
    z = b // 4
    me = s * 16 + b
    core_mate = (s, b + 1 - 2 * c)
    y_mate = (s, b + 2 - 4 * y)
    x_mate = (1 - s, b)

    def zdev(i):
        return (s, ((z + 1 + i) % 4) * 4 + y * 2 + c)

    def copy(src, dst, ss, rs, dev):
        return pltpu.make_async_remote_copy(
            src_ref=src, dst_ref=dst, send_sem=ss, recv_sem=rs,
            device_id=dev, device_id_type=MESH_ID)

    barrier = pltpu.get_barrier_semaphore()

    def greet(k, carry):
        d = (me + k) % 32
        pl.semaphore_signal(barrier, inc=1, device_id=(d // 16, d % 16), device_id_type=MESH_ID)
        return carry

    lax.fori_loop(1, 32, greet, 0)

    row = line_ref[...]
    sub = lax.broadcasted_iota(jnp.int32, (64, 64), 0)
    lane = lax.broadcasted_iota(jnp.int32, (64, 64), 1)
    rows = jnp.broadcast_to(row, (64, 64))
    diag = sub == lane
    col = jnp.sum(jnp.where(diag, rows, 0), axis=1, keepdims=True)
    bus_col = jnp.sum(jnp.where(diag, jnp.broadcast_to(busid_ref[...], (64, 64)), 0), axis=1, keepdims=True)
    owner_row = rows // 3
    owner_col = col // 3
    same = jnp.where((owner_row == owner_col) & (lane < sub), 1, 0)
    rank = jnp.sum(same, axis=1, keepdims=True)
    place = owner_col * 6 + rank
    tcol = lax.broadcasted_iota(jnp.int32, (64, 1), 0)
    code = tcol * 8 + (col - owner_col * 3 + 1) * 2 + bus_col
    slot_ids = lax.broadcasted_iota(jnp.int32, (64, 128), 1)
    table = jnp.sum(jnp.where(place == slot_ids, code, 0), axis=0, keepdims=True)
    table_v[...] = jnp.broadcast_to(table, (8, 128))
    to_smem = pltpu.make_async_copy(table_v, table_s, table_sem)
    to_smem.start()
    pl.semaphore_wait(barrier, 31)

    def inj_copy(k):
        d = (me + k) % 32
        src = (me + 32 - k) % 32
        db = d % 16
        out = copy(inj_ref.at[:, pl.ds(pl.multiple_of(db * 256, 256), 256)],
                   inj_buf.at[me], inj_ss.at[k], inj_rs.at[k], (d // 16, db))
        inn = copy(inj_ref.at[:, pl.ds(pl.multiple_of(db * 256, 256), 256)],
                   inj_buf.at[src], inj_ss.at[k], inj_rs.at[k], (d // 16, db))
        return out, inn

    def inj_start(k, carry):
        inj_copy(k)[0].start()
        return carry

    lax.fori_loop(1, 32, inj_start, 0)
    pred_copy = copy(pred_ref, pred_recv, pred_sem.at[0], pred_sem.at[1], x_mate)
    pred_copy.start()
    inj_buf[me] = inj_ref[:, pl.ds(pl.multiple_of(b * 256, 256), 256)]

    to_smem.wait()

    def build(o, carry):
        tiles = []
        for j in range(6):
            v = table_s[0, o * 6 + j]
            tiles.append((tiles_ref[v // 8].astype(F32), (v // 2) % 4, v % 2))
        for m in range(3):
            for bb in range(2):
                total = jnp.zeros((64, 128), F32)
                for tile, blk, bus in tiles:
                    w = jnp.where((blk == m + 1) & (bus == bb), 1.0, 0.0).astype(F32)
                    total = total + tile * w
                hi = total.astype(BF16)
                lo = (total - hi.astype(F32)).astype(BF16)
                dense[o, 0, pl.ds(m * 64, 64), pl.ds(bb * 128, 128)] = hi
                dense[o, 1, pl.ds(m * 64, 64), pl.ds(bb * 128, 128)] = lo
        return carry

    lax.fori_loop(0, 16, build, 0)

    def inj_wait(k, carry):
        inj_copy(k)[1].wait_recv()
        return carry

    lax.fori_loop(1, 32, inj_wait, 0)
    inj_t[...] = inj_buf[...].astype(F32).reshape(256, 256).T.astype(BF16)

    def forward(o):
        return (jnp.dot(dense[o, 0], inj_t[...], preferred_element_type=F32)
                + jnp.dot(dense[o, 1], inj_t[...], preferred_element_type=F32))

    def owner(k, core):
        far = k // 4
        zz = (z + 1 + k % 4) % 4
        yy = jnp.where(far == 0, 1 - y, y)
        return zz * 4 + yy * 2 + core

    def c_copy(k):
        return copy(csend.at[k], crecv.at[k], c_ss.at[k], c_rs.at[k], core_mate)

    def y_copy(k):
        return copy(ysend.at[k], yrecv.at[k], y_ss.at[k], y_rs.at[k], y_mate)

    def z_copy(i):
        return copy(zsend.at[i], zrecv.at[2 - i], z_ss.at[i], z_rs.at[2 - i], zdev(i))

    def z_arrival(j):
        return copy(zsend.at[j], zrecv.at[j], z_ss.at[j], z_rs.at[j], zdev(j))

    def send_core(k, carry):
        csend[k] = forward(owner(k, 1 - c)).astype(BF16)
        c_copy(k).start()
        return carry

    lax.fori_loop(0, 8, send_core, 0)

    def send_y(k, carry):
        part = forward(owner(k, c))
        c_copy(k).wait_recv()
        ysend[k] = (part + crecv[k].astype(F32)).astype(BF16)
        y_copy(k).start()
        return carry

    lax.fori_loop(0, 4, send_y, 0)

    def keep(k, carry):
        part = forward(owner(k, c))
        c_copy(k).wait_recv()
        acc[k - 4] = part + crecv[k].astype(F32)
        return carry

    lax.fori_loop(4, 8, keep, 0)
    pred_copy.wait_recv()
    mine = pred_ref[...].astype(F32).T
    theirs = pred_recv[...].astype(F32).T
    lim_all = jnp.broadcast_to(lim_ref[...].astype(F32) * 0.01, (128, 384)).T
    first = s == 0
    for m in range(3):
        upper, lower = slice(m * 128, m * 128 + 64), slice(m * 128 + 64, m * 128 + 128)
        a = jnp.where(first, mine[upper], mine[lower])
        d = jnp.where(first, theirs[upper], theirs[lower])
        pred_t[0, pl.ds(m * 64, 64), pl.ds(0, 128)] = jnp.where(first, a, d)
        pred_t[0, pl.ds(m * 64, 64), pl.ds(128, 128)] = jnp.where(first, d, a)
        e = jnp.where(first, lim_all[upper], lim_all[lower])
        pred_t[1, pl.ds(m * 64, 64), pl.ds(0, 128)] = e
        pred_t[1, pl.ds(m * 64, 64), pl.ds(128, 128)] = e

    for i in range(3):
        y_copy(i).wait_recv()
        zsend[i] = (acc[i] + yrecv[i].astype(F32)).astype(BF16)
        z_copy(i).start()

    def turn(o, carry):
        dense_t[o, 0] = dense[o, 0].T
        dense_t[o, 1] = dense[o, 1].T
        return carry

    lax.fori_loop(0, 16, turn, 0)
    y_copy(3).wait_recv()
    flow = acc[3] + yrecv[3].astype(F32)
    for j in range(3):
        z_arrival(j).wait_recv()
        flow = flow + zrecv[j].astype(F32)

    limit = pred_t[1]
    grad = ((flow - pred_t[0]) + jax.nn.sigmoid(4.0 * (flow - limit))
            - jax.nn.sigmoid(4.0 * (-flow - limit)))
    ag[3] = grad.astype(BF16)

    def az_copy(i):
        return copy(ag.at[3], ag.at[2 - i], az_ss.at[i], az_rs.at[2 - i], zdev(i))

    def az_arrival(j):
        return copy(ag.at[3], ag.at[j], az_ss.at[j], az_rs.at[j], zdev(j))

    def ay_copy(i):
        return copy(ag.at[i], ag.at[4 + i], ay_ss.at[i], ay_rs.at[i], y_mate)

    def ac_copy(i):
        return copy(ag.at[i], ag.at[8 + i], ac_ss.at[i], ac_rs.at[i], core_mate)

    for i in range(3):
        az_copy(i).start()
    ay_copy(3).start()
    ac_copy(3).start()
    fx_send[...] = jnp.where(first, flow[:, 128:], flow[:, :128])
    fx_own[...] = jnp.where(first, flow[:, :128], flow[:, 128:])
    fx_copy = copy(fx_send, fx_recv, fx_sem.at[0], fx_sem.at[1], x_mate)
    fx_copy.start()

    def backward(slot):
        zz = (z + 1 + slot % 4) % 4
        yy = (y + slot // 4) % 2
        cc = (c + slot // 8) % 2
        o = zz * 4 + yy * 2 + cc
        return (jnp.dot(dense_t[o, 0], ag[slot], preferred_element_type=F32)
                + jnp.dot(dense_t[o, 1], ag[slot], preferred_element_type=F32))

    total = gx_own
    total[...] = backward(3)

    for i in range(3):
        az_arrival(i).wait_recv()
        ay_copy(i).start()
        ac_copy(i).start()
        total[...] += backward(i)
    for i in (3, 0, 1, 2):
        ay_copy(i).wait_recv()
        ac_copy(4 + i).start()
        total[...] += backward(4 + i)
    for i in (3, 0, 1, 2, 7, 4, 5, 6):
        ac_copy(i).wait_recv()
        total[...] += backward(8 + i)

    whole = total[...]
    gx_send[...] = jnp.where(first, whole[:, 128:], whole[:, :128])
    gx_copy = copy(gx_send, gx_recv, gx_sem.at[0], gx_sem.at[1], x_mate)
    gx_copy.start()

    fx_copy.wait_recv()
    for m in range(3):
        rows_m = pl.ds(m * 64, 64)
        mine_m, other_m = fx_own[rows_m, :], fx_recv[rows_m, :]
        top = jnp.where(first, mine_m, other_m)
        low = jnp.where(first, other_m, mine_m)
        fout_ref[:, pl.ds(m * 128, 128)] = jnp.concatenate([top, low], axis=0).T

    kept = jnp.where(first, whole[:, :128], whole[:, 128:])
    gx_copy.wait_recv()
    gsend[...] = (kept + gx_recv[...]).T.reshape(16, 8, 256).astype(BF16)

    def out_copy(k):
        d = (b + k) % 16
        src = (b + 16 - k) % 16
        out = copy(gsend.at[d], grecv.at[b], out_ss.at[k], out_rs.at[k], (s, d))
        inn = copy(gsend.at[d], grecv.at[src], out_ss.at[k], out_rs.at[k], (s, d))
        return out, inn

    def out_start(k, carry):
        out_copy(k)[0].start()
        return carry

    lax.fori_loop(1, 16, out_start, 0)
    grecv[b] = gsend[b]

    def sent_inj(k, carry):
        inj_copy(k)[0].wait_send()
        return carry

    lax.fori_loop(1, 32, sent_inj, 0)

    def sent_c(k, carry):
        c_copy(k).wait_send()
        ac_copy(k).wait_send()
        return carry

    lax.fori_loop(0, 8, sent_c, 0)

    def sent_y(k, carry):
        y_copy(k).wait_send()
        ay_copy(k).wait_send()
        return carry

    lax.fori_loop(0, 4, sent_y, 0)
    for i in range(3):
        z_copy(i).wait_send()
        az_copy(i).wait_send()
    pred_copy.wait_send()
    fx_copy.wait_send()
    gx_copy.wait_send()

    def out_wait(k, carry):
        out_copy(k)[1].wait_recv()
        return carry

    lax.fori_loop(1, 16, out_wait, 0)
    for k in range(16):
        gout_ref[:, pl.ds(k * 256, 256)] = grecv[k]

    def sent_out(k, carry):
        out_copy(k)[0].wait_send()
        return carry

    lax.fori_loop(1, 16, sent_out, 0)


def fused(injections, tile_values, tile_line, tile_bus, flow_pred, line_limit):
    vmem = pl.BlockSpec(memory_space=pltpu.VMEM)
    dma = pltpu.SemaphoreType.DMA
    block = (192, 256)
    return pl.pallas_call(
        kernel,
        out_shape=(jax.ShapeDtypeStruct((8, 4096), BF16), jax.ShapeDtypeStruct((128, 384), F32)),
        in_specs=[vmem] * 6,
        out_specs=(vmem, vmem),
        scratch_shapes=[
            pltpu.VMEM((8, 128), jnp.int32),
            pltpu.SMEM((8, 128), jnp.int32),
            pltpu.VMEM((32, 8, 256), BF16),
            pltpu.VMEM((256, 256), BF16),
            pltpu.VMEM((16, 2) + block, BF16),
            pltpu.VMEM((16, 2, 256, 192), BF16),
            pltpu.VMEM((8,) + block, BF16),
            pltpu.VMEM((8,) + block, BF16),
            pltpu.VMEM((4,) + block, BF16),
            pltpu.VMEM((4,) + block, BF16),
            pltpu.VMEM((4,) + block, F32),
            pltpu.VMEM((3,) + block, BF16),
            pltpu.VMEM((3,) + block, BF16),
            pltpu.VMEM((128, 384), BF16),
            pltpu.VMEM((2,) + block, F32),
            pltpu.VMEM((192, 128), F32),
            pltpu.VMEM((192, 128), F32),
            pltpu.VMEM((192, 128), F32),
            pltpu.VMEM((16,) + block, BF16),
            pltpu.VMEM((256, 128), F32),
            pltpu.VMEM((256, 256), F32),
            pltpu.VMEM((256, 128), F32),
            pltpu.VMEM((16, 8, 256), BF16),
            pltpu.VMEM((16, 8, 256), BF16),
            dma, dma((32,)), dma((32,)), dma((2,)),
            dma((8,)), dma((8,)), dma((4,)), dma((4,)), dma((3,)), dma((3,)),
            dma((2,)), dma((3,)), dma((3,)), dma((4,)), dma((4,)), dma((8,)), dma((8,)),
            dma((2,)), dma((16,)), dma((16,)),
        ],
        compiler_params=pltpu.CompilerParams(
            collective_id=0, has_side_effects=True, vmem_limit_bytes=48 * 1024 * 1024),
    )(injections, tile_values, tile_line.reshape(1, -1), tile_bus.reshape(1, -1), flow_pred,
      line_limit.reshape(1, -1))


def per_device(injections, tile_values, tile_line, tile_bus, flow_pred, line_limit):
    bus_count = lax.axis_size("bus")
    local_inj = lax.all_to_all(injections, "bus", split_axis=1, concat_axis=0, tiled=True)
    tile_full = lax.all_gather(tile_values, "scen", axis=1, tiled=True)
    tile_count = tile_full.shape[0]
    tile_size = tile_full.shape[1]
    row_count = local_inj.shape[0]
    blocks_here = local_inj.shape[1] // tile_size
    line_blocks = flow_pred.shape[1] // tile_size
    per_owner = tile_count // bus_count
    capacity = per_owner + max(1, tile_count // (2 * bus_count))
    slot_total = bus_count * capacity
    inj_blocks = local_inj.reshape(row_count, blocks_here, tile_size)
    per_tile_inj = jnp.take(inj_blocks, tile_bus, axis=1)
    partial_flows = jnp.einsum(
        "stb,tlb->tsl", per_tile_inj, tile_full, preferred_element_type=jnp.float32
    )
    owner_index = tile_line // line_blocks
    within_owner = tile_line % line_blocks
    owner_hits = (owner_index[:, None] == jnp.arange(bus_count, dtype=jnp.int32)[None, :]).astype(
        jnp.int32
    )
    rank_within = jnp.sum(jnp.cumsum(owner_hits, axis=0) * owner_hits, axis=1) - 1
    slot_index = owner_index * capacity + rank_within
    send_buffer = (
        jnp.zeros((slot_total, row_count, tile_size), jnp.float32).at[slot_index].set(partial_flows)
    )
    slot_label = jnp.full((slot_total,), -1, jnp.int32).at[slot_index].set(within_owner)
    received, received_label = (
        lax.all_to_all(send_buffer, "bus", split_axis=0, concat_axis=0, tiled=True),
        lax.all_to_all(slot_label, "bus", split_axis=0, concat_axis=0, tiled=True),
    )
    select_mask = (
        received_label[None, :] == jnp.arange(line_blocks, dtype=jnp.int32)[:, None]
    ).astype(jnp.float32)
    flow_blocks = jnp.einsum("ms,srl->rml", select_mask, received, precision=lax.Precision.HIGHEST)
    flows = flow_blocks.reshape(row_count, line_blocks * tile_size)
    line_cap = line_limit.astype(jnp.float32) * 0.01
    residual = flows - flow_pred.astype(jnp.float32)
    grad_flow = (
        residual
        + jax.nn.sigmoid(4.0 * (flows - line_cap))
        - jax.nn.sigmoid(4.0 * (-flows - line_cap))
    ).astype(jnp.bfloat16)
    gathered = lax.all_gather(grad_flow, "bus", axis=1, tiled=True)
    gathered_blocks = gathered.reshape(row_count, gathered.shape[1] // tile_size, tile_size)
    per_tile_grad = jnp.take(gathered_blocks, tile_line, axis=1)
    contrib = jnp.einsum(
        "stl,tlb->stb", per_tile_grad, tile_full, preferred_element_type=jnp.float32
    )
    bus_select = (tile_bus[:, None] == jnp.arange(blocks_here, dtype=jnp.int32)[None, :]).astype(
        jnp.float32
    )
    grad_blocks_bus = jnp.einsum(
        "stb,tk->skb", contrib, bus_select, precision=lax.Precision.HIGHEST
    )
    grad_local = grad_blocks_bus.reshape(row_count, blocks_here * tile_size).astype(jnp.bfloat16)
    grad_injections = lax.all_to_all(grad_local, "bus", split_axis=0, concat_axis=1, tiled=True)
    return (grad_injections, flows)


def solution(mesh):
    small = mesh.shape["scen"] == 2 and mesh.shape["bus"] == 16
    return jax.shard_map(
        fused if small else per_device,
        mesh=mesh,
        in_specs=(
            P(("scen", "bus"), None),
            P("bus", "scen", None),
            P("bus"),
            P("bus"),
            P("scen", "bus"),
            P("bus"),
        ),
        out_specs=(P(("scen", "bus"), None), P("scen", "bus")),
        check_vma=False,
    )
```

```python
import jax
import jax.numpy as jnp
from jax import lax
from jax.experimental import pallas as pl
from jax.experimental.pallas import tpu as pltpu
from jax.sharding import PartitionSpec as P

MESH_ID = pl.DeviceIdType.MESH
F32 = jnp.float32
BF16 = jnp.bfloat16


def kernel(inj_hbm, tiles_hbm, line_hbm, busid_hbm, pred_hbm, lim_hbm, gout_ref, fout_ref,
           inj_ref, tiles_ref, line_ref, busid_ref, pred_ref, lim_ref,
           table_v, table_s, inj_buf, inj_t, dense, dense_t,
           csend, crecv, ysend, yrecv, stash, acc, zsend, zrecv,
           pred_recv, pred_t, flow_t, fx_recv,
           ag, total, gx_recv, gsend, grecv,
           in_sem, table_sem, inj_ss, inj_rs, pred_sem, c_ss, c_rs, y_ss, y_rs, z_ss, z_rs,
           fx_sem, az_ss, az_rs, ay_ss, ay_rs, ac_ss, ac_rs, gx_sem, out_ss, out_rs):
    s = lax.axis_index("scen")
    b = lax.axis_index("bus")
    c = b % 2
    y = (b // 2) % 2
    z = b // 4
    me = s * 16 + b
    core_mate = (s, b + 1 - 2 * c)
    y_mate = (s, b + 2 - 4 * y)
    x_mate = (1 - s, b)
    first = s == 0

    loads = [pltpu.make_async_copy(src, dst, in_sem.at[n]) for n, (src, dst) in enumerate((
        (line_hbm, line_ref), (busid_hbm, busid_ref), (tiles_hbm, tiles_ref),
        (inj_hbm, inj_ref), (pred_hbm, pred_ref), (lim_hbm, lim_ref)))]
    for load in loads:
        load.start()

    def zdev(i):
        return (s, ((z + 1 + i) % 4) * 4 + y * 2 + c)

    def copy(src, dst, ss, rs, dev):
        return pltpu.make_async_remote_copy(
            src_ref=src, dst_ref=dst, send_sem=ss, recv_sem=rs,
            device_id=dev, device_id_type=MESH_ID)

    barrier = pltpu.get_barrier_semaphore()

    def greet(k, carry):
        d = (me + k) % 32
        pl.semaphore_signal(barrier, inc=1, device_id=(d // 16, d % 16), device_id_type=MESH_ID)
        return carry

    lax.fori_loop(1, 32, greet, 0)

    loads[0].wait()
    loads[1].wait()
    row = line_ref[...]
    sub = lax.broadcasted_iota(jnp.int32, (64, 64), 0)
    lane = lax.broadcasted_iota(jnp.int32, (64, 64), 1)
    rows = jnp.broadcast_to(row, (64, 64))
    diag = sub == lane
    col = jnp.sum(jnp.where(diag, rows, 0), axis=1, keepdims=True)
    bus_col = jnp.sum(jnp.where(diag, jnp.broadcast_to(busid_ref[...], (64, 64)), 0), axis=1, keepdims=True)
    owner_row = rows // 3
    owner_col = col // 3
    same = jnp.where((owner_row == owner_col) & (lane < sub), 1, 0)
    rank = jnp.sum(same, axis=1, keepdims=True)
    place = owner_col * 6 + rank
    tcol = lax.broadcasted_iota(jnp.int32, (64, 1), 0)
    code = tcol * 8 + (col - owner_col * 3 + 1) * 2 + bus_col
    slot_ids = lax.broadcasted_iota(jnp.int32, (64, 128), 1)
    table = jnp.sum(jnp.where(place == slot_ids, code, 0), axis=0, keepdims=True)
    table_v[...] = jnp.broadcast_to(table, (8, 128))
    to_smem = pltpu.make_async_copy(table_v, table_s, table_sem)
    to_smem.start()
    pl.semaphore_wait(barrier, 31)

    def inj_copy(k):
        d = (me + k) % 32
        src = (me + 32 - k) % 32
        db = d % 16
        out = copy(inj_hbm.at[:, pl.ds(pl.multiple_of(db * 256, 256), 256)],
                   inj_buf.at[me], inj_ss.at[k], inj_rs.at[k], (d // 16, db))
        inn = copy(inj_hbm.at[:, pl.ds(pl.multiple_of(db * 256, 256), 256)],
                   inj_buf.at[src], inj_ss.at[k], inj_rs.at[k], (d // 16, db))
        return out, inn

    def inj_start(k, carry):
        inj_copy(k)[0].start()
        return carry

    lax.fori_loop(1, 32, inj_start, 0)
    pred_copy = copy(pred_hbm, pred_recv, pred_sem.at[0], pred_sem.at[1], x_mate)
    pred_copy.start()
    loads[3].wait()
    inj_buf[me] = inj_ref[:, pl.ds(pl.multiple_of(b * 256, 256), 256)]

    to_smem.wait()
    loads[2].wait()

    def build(o, carry):
        tiles = []
        for j in range(6):
            v = table_s[0, o * 6 + j]
            tiles.append((tiles_ref[v // 8].astype(F32), (v // 2) % 4, v % 2))
        for m in range(3):
            for bb in range(2):
                total = jnp.zeros((64, 128), F32)
                for tile, blk, bus in tiles:
                    w = jnp.where((blk == m + 1) & (bus == bb), 1.0, 0.0).astype(F32)
                    total = total + tile * w
                hi = total.astype(BF16)
                lo = (total - hi.astype(F32)).astype(BF16)
                dense[o, 0, pl.ds(m * 64, 64), pl.ds(bb * 128, 128)] = hi
                dense[o, 1, pl.ds(m * 64, 64), pl.ds(bb * 128, 128)] = lo
        return carry

    lax.fori_loop(0, 16, build, 0)

    def inj_wait(k, carry):
        inj_copy(k)[1].wait_recv()
        return carry

    lax.fori_loop(1, 32, inj_wait, 0)
    turned = inj_buf[...].astype(F32).reshape(256, 256).T.astype(BF16)
    inj_t[...] = jnp.where(first, jnp.concatenate([turned[:, 128:], turned[:, :128]], axis=1), turned)

    def forward(o):
        return (jnp.dot(dense[o, 0], inj_t[...], preferred_element_type=F32)
                + jnp.dot(dense[o, 1], inj_t[...], preferred_element_type=F32))

    def owner(k, core):
        far = k // 4
        zz = (z + 1 + k % 4) % 4
        yy = jnp.where(far == 0, 1 - y, y)
        return zz * 4 + yy * 2 + core

    def c_copy(h, k):
        return copy(csend.at[h, k], crecv.at[h, k], c_ss.at[h, k], c_rs.at[h, k], core_mate)

    def y_copy(h, k):
        return copy(ysend.at[h, k], yrecv.at[h, k], y_ss.at[h, k], y_rs.at[h, k], y_mate)

    def z_copy(h, i):
        return copy(zsend.at[h, i], zrecv.at[h, 2 - i], z_ss.at[h, i], z_rs.at[h, 2 - i], zdev(i))

    def z_arrival(h, j):
        return copy(zsend.at[h, j], zrecv.at[h, j], z_ss.at[h, j], z_rs.at[h, j], zdev(j))

    def send_core(k, carry):
        part = forward(owner(k, 1 - c)).astype(BF16)
        csend[0, k] = part[:, :128]
        c_copy(0, k).start()
        csend[1, k] = part[:, 128:]
        c_copy(1, k).start()
        return carry

    def send_y(k, carry):
        part = forward(owner(k, c))
        stash[k] = part[:, 128:]
        c_copy(0, k).wait_recv()
        ysend[0, k] = (part[:, :128] + crecv[0, k].astype(F32)).astype(BF16)
        y_copy(0, k).start()
        return carry

    def send_y_late(k, carry):
        c_copy(1, k).wait_recv()
        ysend[1, k] = (stash[k] + crecv[1, k].astype(F32)).astype(BF16)
        y_copy(1, k).start()
        return carry

    def keep(k, carry):
        part = forward(owner(k, c))
        c_copy(0, k).wait_recv()
        acc[0, k - 4] = part[:, :128] + crecv[0, k].astype(F32)
        c_copy(1, k).wait_recv()
        acc[1, k - 4] = part[:, 128:] + crecv[1, k].astype(F32)
        return carry

    def turn(o, carry):
        dense_t[o, 0] = dense[o, 0].T
        dense_t[o, 1] = dense[o, 1].T
        return carry

    def send_z(h):
        for i in range(3):
            y_copy(h, i).wait_recv()
            zsend[h, i] = (acc[h, i] + yrecv[h, i].astype(F32)).astype(BF16)
            z_copy(h, i).start()

    lax.fori_loop(0, 4, send_core, 0)
    lax.fori_loop(0, 4, send_y, 0)
    lax.fori_loop(4, 8, send_core, 0)
    lax.fori_loop(0, 4, send_y_late, 0)
    lax.fori_loop(4, 8, keep, 0)
    send_z(0)
    loads[4].wait()
    loads[5].wait()
    pred_copy.wait_recv()
    mine = pred_ref[...].astype(F32).T
    theirs = pred_recv[...].astype(F32).T
    lim_all = jnp.broadcast_to(lim_ref[...].astype(F32) * 0.01, (128, 384)).T
    for m in range(3):
        upper, lower = slice(m * 128, m * 128 + 64), slice(m * 128 + 64, m * 128 + 128)
        for n, array in enumerate((theirs, mine, lim_all)):
            pred_t[n, pl.ds(m * 64, 64), :] = jnp.where(first, array[upper], array[lower])
    send_z(1)
    lax.fori_loop(0, 16, turn, 0)

    def az_copy(h, i):
        return copy(ag.at[h, 3], ag.at[h, 2 - i], az_ss.at[h, i], az_rs.at[h, 2 - i], zdev(i))

    def az_arrival(h, j):
        return copy(ag.at[h, 3], ag.at[h, j], az_ss.at[h, j], az_rs.at[h, j], zdev(j))

    def ay_copy(h, i):
        return copy(ag.at[h, i], ag.at[h, 4 + i], ay_ss.at[h, i], ay_rs.at[h, i], y_mate)

    def ac_copy(h, i):
        return copy(ag.at[h, i], ag.at[h, 8 + i], ac_ss.at[h, i], ac_rs.at[h, i], core_mate)

    def finish(h):
        y_copy(h, 3).wait_recv()
        flow = acc[h, 3] + yrecv[h, 3].astype(F32)
        for j in range(3):
            z_arrival(h, j).wait_recv()
            flow = flow + zrecv[h, j].astype(F32)
        flow_t[h] = flow
        limit = pred_t[2]
        grad = ((flow - pred_t[h]) + jax.nn.sigmoid(4.0 * (flow - limit))
                - jax.nn.sigmoid(4.0 * (-flow - limit)))
        ag[h, 3] = grad.astype(BF16)
        for i in range(3):
            az_copy(h, i).start()
        ay_copy(h, 3).start()
        ac_copy(h, 3).start()

    def pass_z(h):
        for i in range(3):
            az_arrival(h, i).wait_recv()
            ay_copy(h, i).start()
            ac_copy(h, i).start()

    def pass_y(h):
        for i in (3, 0, 1, 2):
            ay_copy(h, i).wait_recv()
            ac_copy(h, 4 + i).start()

    def backward(h, slot):
        zz = (z + 1 + slot % 4) % 4
        yy = (y + slot // 4) % 2
        cc = (c + slot // 8) % 2
        o = zz * 4 + yy * 2 + cc
        return (jnp.dot(dense_t[o, 0], ag[h, slot], preferred_element_type=F32)
                + jnp.dot(dense_t[o, 1], ag[h, slot], preferred_element_type=F32))

    def add_own(h):
        def step(k, carry):
            total[h] += backward(h, k)
            return carry
        total[h] = jnp.zeros((256, 128), F32)
        lax.fori_loop(0, 8, step, 0)

    def add_core(h):
        for i in (3, 0, 1, 2, 7, 4, 5, 6):
            ac_copy(h, i).wait_recv()
            total[h] += backward(h, 8 + i)

    finish(0)
    fx_copy = copy(flow_t.at[0], fx_recv, fx_sem.at[0], fx_sem.at[1], x_mate)
    fx_copy.start()
    finish(1)
    pass_z(0)
    pass_y(0)
    pass_z(1)
    add_own(0)
    add_core(0)
    gx_copy = copy(total.at[0], gx_recv, gx_sem.at[0], gx_sem.at[1], x_mate)
    gx_copy.start()
    pass_y(1)
    add_own(1)
    add_core(1)
    gx_copy.wait_recv()
    gsend[...] = (total[1] + gx_recv[...]).T.reshape(16, 8, 256).astype(BF16)

    def out_copy(k):
        d = (b + k) % 16
        src = (b + 16 - k) % 16
        out = copy(gsend.at[d], grecv.at[b], out_ss.at[k], out_rs.at[k], (s, d))
        inn = copy(gsend.at[d], grecv.at[src], out_ss.at[k], out_rs.at[k], (s, d))
        return out, inn

    def out_start(k, carry):
        out_copy(k)[0].start()
        return carry

    lax.fori_loop(1, 16, out_start, 0)
    grecv[b] = gsend[b]

    fx_copy.wait_recv()
    for m in range(3):
        rows_m = pl.ds(m * 64, 64)
        mine_m, other_m = flow_t[1, rows_m, :], fx_recv[rows_m, :]
        top = jnp.where(first, mine_m, other_m)
        low = jnp.where(first, other_m, mine_m)
        fout_ref[:, pl.ds(m * 128, 128)] = jnp.concatenate([top, low], axis=0).T

    def sent_inj(k, carry):
        inj_copy(k)[0].wait_send()
        return carry

    lax.fori_loop(1, 32, sent_inj, 0)

    for h in range(2):
        def sent_c(k, carry):
            c_copy(h, k).wait_send()
            ac_copy(h, k).wait_send()
            return carry

        lax.fori_loop(0, 8, sent_c, 0)

        def sent_y(k, carry):
            y_copy(h, k).wait_send()
            ay_copy(h, k).wait_send()
            return carry

        lax.fori_loop(0, 4, sent_y, 0)
        for i in range(3):
            z_copy(h, i).wait_send()
            az_copy(h, i).wait_send()
    pred_copy.wait_send()
    fx_copy.wait_send()
    gx_copy.wait_send()

    def out_wait(k, carry):
        out_copy(k)[1].wait_recv()
        return carry

    lax.fori_loop(1, 16, out_wait, 0)
    for k in range(16):
        gout_ref[:, pl.ds(k * 256, 256)] = grecv[k]

    def sent_out(k, carry):
        out_copy(k)[0].wait_send()
        return carry

    lax.fori_loop(1, 16, sent_out, 0)


def fused(injections, tile_values, tile_line, tile_bus, flow_pred, line_limit):
    vmem = pl.BlockSpec(memory_space=pltpu.VMEM)
    dma = pltpu.SemaphoreType.DMA
    block, half = (192, 256), (192, 128)
    return pl.pallas_call(
        kernel,
        out_shape=(jax.ShapeDtypeStruct((8, 4096), BF16), jax.ShapeDtypeStruct((128, 384), F32)),
        in_specs=[pl.BlockSpec(memory_space=pl.ANY)] * 6,
        out_specs=(vmem, vmem),
        scratch_shapes=[
            pltpu.VMEM((8, 4096), BF16),
            pltpu.VMEM((64, 64, 128), BF16),
            pltpu.VMEM((1, 64), jnp.int32),
            pltpu.VMEM((1, 64), jnp.int32),
            pltpu.VMEM((128, 384), BF16),
            pltpu.VMEM((1, 384), jnp.int32),
            pltpu.VMEM((8, 128), jnp.int32),
            pltpu.SMEM((8, 128), jnp.int32),
            pltpu.VMEM((32, 8, 256), BF16),
            pltpu.VMEM((256, 256), BF16),
            pltpu.VMEM((16, 2) + block, BF16),
            pltpu.VMEM((16, 2, 256, 192), BF16),
            pltpu.VMEM((2, 8) + half, BF16),
            pltpu.VMEM((2, 8) + half, BF16),
            pltpu.VMEM((2, 4) + half, BF16),
            pltpu.VMEM((2, 4) + half, BF16),
            pltpu.VMEM((4,) + half, F32),
            pltpu.VMEM((2, 4) + half, F32),
            pltpu.VMEM((2, 3) + half, BF16),
            pltpu.VMEM((2, 3) + half, BF16),
            pltpu.VMEM((128, 384), BF16),
            pltpu.VMEM((3,) + half, F32),
            pltpu.VMEM((2,) + half, F32),
            pltpu.VMEM(half, F32),
            pltpu.VMEM((2, 16) + half, BF16),
            pltpu.VMEM((2, 256, 128), F32),
            pltpu.VMEM((256, 128), F32),
            pltpu.VMEM((16, 8, 256), BF16),
            pltpu.VMEM((16, 8, 256), BF16),
            dma((6,)), dma, dma((32,)), dma((32,)), dma((2,)),
            dma((2, 8)), dma((2, 8)), dma((2, 4)), dma((2, 4)), dma((2, 3)), dma((2, 3)),
            dma((2,)), dma((2, 3)), dma((2, 3)), dma((2, 4)), dma((2, 4)), dma((2, 8)), dma((2, 8)),
            dma((2,)), dma((16,)), dma((16,)),
        ],
        compiler_params=pltpu.CompilerParams(
            collective_id=0, has_side_effects=True, vmem_limit_bytes=56 * 1024 * 1024),
    )(injections, tile_values, tile_line.reshape(1, -1), tile_bus.reshape(1, -1), flow_pred,
      line_limit.reshape(1, -1))


def per_device(injections, tile_values, tile_line, tile_bus, flow_pred, line_limit):
    bus_count = lax.axis_size("bus")
    local_inj = lax.all_to_all(injections, "bus", split_axis=1, concat_axis=0, tiled=True)
    tile_full = lax.all_gather(tile_values, "scen", axis=1, tiled=True)
    tile_count = tile_full.shape[0]
    tile_size = tile_full.shape[1]
    row_count = local_inj.shape[0]
    blocks_here = local_inj.shape[1] // tile_size
    line_blocks = flow_pred.shape[1] // tile_size
    per_owner = tile_count // bus_count
    capacity = per_owner + max(1, tile_count // (2 * bus_count))
    slot_total = bus_count * capacity
    inj_blocks = local_inj.reshape(row_count, blocks_here, tile_size)
    per_tile_inj = jnp.take(inj_blocks, tile_bus, axis=1)
    partial_flows = jnp.einsum(
        "stb,tlb->tsl", per_tile_inj, tile_full, preferred_element_type=jnp.float32
    )
    owner_index = tile_line // line_blocks
    within_owner = tile_line % line_blocks
    owner_hits = (owner_index[:, None] == jnp.arange(bus_count, dtype=jnp.int32)[None, :]).astype(
        jnp.int32
    )
    rank_within = jnp.sum(jnp.cumsum(owner_hits, axis=0) * owner_hits, axis=1) - 1
    slot_index = owner_index * capacity + rank_within
    send_buffer = (
        jnp.zeros((slot_total, row_count, tile_size), jnp.float32).at[slot_index].set(partial_flows)
    )
    slot_label = jnp.full((slot_total,), -1, jnp.int32).at[slot_index].set(within_owner)
    received, received_label = (
        lax.all_to_all(send_buffer, "bus", split_axis=0, concat_axis=0, tiled=True),
        lax.all_to_all(slot_label, "bus", split_axis=0, concat_axis=0, tiled=True),
    )
    select_mask = (
        received_label[None, :] == jnp.arange(line_blocks, dtype=jnp.int32)[:, None]
    ).astype(jnp.float32)
    flow_blocks = jnp.einsum("ms,srl->rml", select_mask, received, precision=lax.Precision.HIGHEST)
    flows = flow_blocks.reshape(row_count, line_blocks * tile_size)
    line_cap = line_limit.astype(jnp.float32) * 0.01
    residual = flows - flow_pred.astype(jnp.float32)
    grad_flow = (
        residual
        + jax.nn.sigmoid(4.0 * (flows - line_cap))
        - jax.nn.sigmoid(4.0 * (-flows - line_cap))
    ).astype(jnp.bfloat16)
    gathered = lax.all_gather(grad_flow, "bus", axis=1, tiled=True)
    gathered_blocks = gathered.reshape(row_count, gathered.shape[1] // tile_size, tile_size)
    per_tile_grad = jnp.take(gathered_blocks, tile_line, axis=1)
    contrib = jnp.einsum(
        "stl,tlb->stb", per_tile_grad, tile_full, preferred_element_type=jnp.float32
    )
    bus_select = (tile_bus[:, None] == jnp.arange(blocks_here, dtype=jnp.int32)[None, :]).astype(
        jnp.float32
    )
    grad_blocks_bus = jnp.einsum(
        "stb,tk->skb", contrib, bus_select, precision=lax.Precision.HIGHEST
    )
    grad_local = grad_blocks_bus.reshape(row_count, blocks_here * tile_size).astype(jnp.bfloat16)
    grad_injections = lax.all_to_all(grad_local, "bus", split_axis=0, concat_axis=1, tiled=True)
    return (grad_injections, flows)


def solution(mesh):
    small = mesh.shape["scen"] == 2 and mesh.shape["bus"] == 16
    return jax.shard_map(
        fused if small else per_device,
        mesh=mesh,
        in_specs=(
            P(("scen", "bus"), None),
            P("bus", "scen", None),
            P("bus"),
            P("bus"),
            P("scen", "bus"),
            P("bus"),
        ),
        out_specs=(P(("scen", "bus"), None), P("scen", "bus")),
        check_vma=False,
    )
```

```python
import jax
import jax.numpy as jnp
from jax import lax
from jax.experimental import pallas as pl
from jax.experimental.pallas import tpu as pltpu
from jax.sharding import PartitionSpec as P

MESH_ID = pl.DeviceIdType.MESH
F32 = jnp.float32
BF16 = jnp.bfloat16


def kernel(inj_hbm, tiles_hbm, line_hbm, busid_hbm, pred_hbm, lim_hbm, gout_ref, fout_ref,
           inj_ref, tiles_ref, line_ref, busid_ref, pred_ref, lim_ref,
           table_v, table_s, inj_buf, inj_t, dense, dense_t,
           csend, crecv, ysend, yrecv, stash, acc, zsend, zrecv,
           pred_recv, pred_t, flow_t, fx_recv,
           ag, total, gx_recv, gsend, grecv,
           in_sem, table_sem, inj_ss, inj_rs, pred_sem, c_ss, c_rs, y_ss, y_rs, z_ss, z_rs,
           fx_sem, az_ss, az_rs, ay_ss, ay_rs, ac_ss, ac_rs, gx_sem, out_ss, out_rs):
    s = lax.axis_index("scen")
    b = lax.axis_index("bus")
    c = b % 2
    y = (b // 2) % 2
    z = b // 4
    me = s * 16 + b
    core_mate = (s, b + 1 - 2 * c)
    y_mate = (s, b + 2 - 4 * y)
    x_mate = (1 - s, b)
    first = s == 0

    loads = [pltpu.make_async_copy(src, dst, in_sem.at[n]) for n, (src, dst) in enumerate((
        (line_hbm, line_ref), (busid_hbm, busid_ref), (tiles_hbm, tiles_ref),
        (inj_hbm, inj_ref), (pred_hbm, pred_ref), (lim_hbm, lim_ref)))]
    for load in loads:
        load.start()

    def zdev(i):
        return (s, ((z + 1 + i) % 4) * 4 + y * 2 + c)

    def copy(src, dst, ss, rs, dev):
        return pltpu.make_async_remote_copy(
            src_ref=src, dst_ref=dst, send_sem=ss, recv_sem=rs,
            device_id=dev, device_id_type=MESH_ID)

    barrier = pltpu.get_barrier_semaphore()

    def greet(k, carry):
        d = (me + k) % 32
        pl.semaphore_signal(barrier, inc=1, device_id=(d // 16, d % 16), device_id_type=MESH_ID)
        return carry

    lax.fori_loop(1, 32, greet, 0)

    loads[0].wait()
    loads[1].wait()
    row = line_ref[...]
    sub = lax.broadcasted_iota(jnp.int32, (64, 64), 0)
    lane = lax.broadcasted_iota(jnp.int32, (64, 64), 1)
    rows = jnp.broadcast_to(row, (64, 64))
    diag = sub == lane
    col = jnp.sum(jnp.where(diag, rows, 0), axis=1, keepdims=True)
    bus_col = jnp.sum(jnp.where(diag, jnp.broadcast_to(busid_ref[...], (64, 64)), 0), axis=1, keepdims=True)
    owner_row = rows // 3
    owner_col = col // 3
    same = jnp.where((owner_row == owner_col) & (lane < sub), 1, 0)
    rank = jnp.sum(same, axis=1, keepdims=True)
    place = owner_col * 6 + rank
    tcol = lax.broadcasted_iota(jnp.int32, (64, 1), 0)
    code = tcol * 8 + (col - owner_col * 3 + 1) * 2 + bus_col
    slot_ids = lax.broadcasted_iota(jnp.int32, (64, 128), 1)
    table = jnp.sum(jnp.where(place == slot_ids, code, 0), axis=0, keepdims=True)
    table_v[...] = jnp.broadcast_to(table, (8, 128))
    to_smem = pltpu.make_async_copy(table_v, table_s, table_sem)
    to_smem.start()
    pl.semaphore_wait(barrier, 31)

    def inj_copy(k):
        d = (me + k) % 32
        src = (me + 32 - k) % 32
        db = d % 16
        out = copy(inj_hbm.at[:, pl.ds(pl.multiple_of(db * 256, 256), 256)],
                   inj_buf.at[me], inj_ss.at[k], inj_rs.at[k], (d // 16, db))
        inn = copy(inj_hbm.at[:, pl.ds(pl.multiple_of(db * 256, 256), 256)],
                   inj_buf.at[src], inj_ss.at[k], inj_rs.at[k], (d // 16, db))
        return out, inn

    def inj_start(k, carry):
        inj_copy(k)[0].start()
        return carry

    lax.fori_loop(1, 32, inj_start, 0)
    pred_copy = copy(pred_hbm, pred_recv, pred_sem.at[0], pred_sem.at[1], x_mate)
    pred_copy.start()
    loads[3].wait()
    inj_buf[me] = inj_ref[:, pl.ds(pl.multiple_of(b * 256, 256), 256)]

    to_smem.wait()
    loads[2].wait()

    def build(r, carry):
        zz = (z + 1 + r % 4) % 4
        yy = (y + (r // 4) % 2) % 2
        cc = (c + r // 8) % 2
        o = zz * 4 + yy * 2 + cc
        tiles = []
        for j in range(6):
            v = table_s[0, o * 6 + j]
            tiles.append((tiles_ref[v // 8].astype(F32), (v // 2) % 4, v % 2))
        for m in range(3):
            for bb in range(2):
                part = jnp.zeros((64, 128), F32)
                for tile, blk, bus in tiles:
                    w = jnp.where((blk == m + 1) & (bus == bb), 1.0, 0.0).astype(F32)
                    part = part + tile * w
                dense[r, pl.ds(m * 64, 64), pl.ds(bb * 128, 128)] = part.astype(BF16)
        return carry

    lax.fori_loop(0, 16, build, 0)

    def inj_wait(k, carry):
        inj_copy(k)[1].wait_recv()
        return carry

    lax.fori_loop(1, 32, inj_wait, 0)
    turned = inj_buf[...].astype(F32).reshape(256, 256).T.astype(BF16)
    inj_t[...] = jnp.where(first, jnp.concatenate([turned[:, 128:], turned[:, :128]], axis=1), turned)

    def forward(group):
        rows = dense[pl.ds(group * 4, 4)].reshape(768, 256)
        return jnp.dot(rows, inj_t[...], preferred_element_type=F32).reshape(4, 192, 256)

    def c_copy(h, k):
        return copy(csend.at[h, k], crecv.at[h, k], c_ss.at[h, k], c_rs.at[h, k], core_mate)

    def y_copy(h, k):
        return copy(ysend.at[h, k], yrecv.at[h, k], y_ss.at[h, k], y_rs.at[h, k], y_mate)

    def z_copy(h, i):
        return copy(zsend.at[h, i], zrecv.at[h, 2 - i], z_ss.at[h, i], z_rs.at[h, 2 - i], zdev(i))

    def z_arrival(h, j):
        return copy(zsend.at[h, j], zrecv.at[h, j], z_ss.at[h, j], z_rs.at[h, j], zdev(j))

    def send_core(group):
        part = forward(2 + group).astype(BF16)
        for h in range(2):
            for i in range(4):
                csend[h, group * 4 + i] = part[i, :, h * 128:h * 128 + 128]
                c_copy(h, group * 4 + i).start()

    def turn(group):
        dense_t[group] = dense[pl.ds(group * 4, 4)].reshape(768, 256).T

    def send_z(h, i):
        y_copy(h, i).wait_recv()
        zsend[h, i] = (acc[h, i] + yrecv[h, i].astype(F32)).astype(BF16)
        z_copy(h, i).start()

    send_core(1)
    far = forward(1)
    for i in range(4):
        stash[i] = far[i, :, 128:]
        c_copy(0, 4 + i).wait_recv()
        ysend[0, i] = (far[i, :, :128] + crecv[0, 4 + i].astype(F32)).astype(BF16)
        y_copy(0, i).start()
    send_core(0)
    for i in range(4):
        c_copy(1, 4 + i).wait_recv()
        ysend[1, i] = (stash[i] + crecv[1, 4 + i].astype(F32)).astype(BF16)
        y_copy(1, i).start()
    near = forward(0)
    for h in range(2):
        for i in range(4):
            c_copy(h, i).wait_recv()
            acc[h, i] = near[i, :, h * 128:h * 128 + 128] + crecv[h, i].astype(F32)
    for i in range(3):
        send_z(0, i)
        turn(i)
    loads[4].wait()
    loads[5].wait()
    pred_copy.wait_recv()
    mine = pred_ref[...].astype(F32).T
    theirs = pred_recv[...].astype(F32).T
    lim_all = jnp.broadcast_to(lim_ref[...].astype(F32)[None, :] * 0.01, (128, 384)).T
    for m in range(3):
        upper, lower = slice(m * 128, m * 128 + 64), slice(m * 128 + 64, m * 128 + 128)
        for n, array in enumerate((theirs, mine, lim_all)):
            pred_t[n, pl.ds(m * 64, 64), :] = jnp.where(first, array[upper], array[lower])
    for i in range(3):
        send_z(1, i)
    turn(3)

    def az_copy(h, i):
        return copy(ag.at[h, 3], ag.at[h, 2 - i], az_ss.at[h, i], az_rs.at[h, 2 - i], zdev(i))

    def az_arrival(h, j):
        return copy(ag.at[h, 3], ag.at[h, j], az_ss.at[h, j], az_rs.at[h, j], zdev(j))

    def ay_copy(h, i):
        return copy(ag.at[h, i], ag.at[h, 4 + i], ay_ss.at[h, i], ay_rs.at[h, i], y_mate)

    def ac_copy(h, i):
        return copy(ag.at[h, i], ag.at[h, 8 + i], ac_ss.at[h, i], ac_rs.at[h, i], core_mate)

    def finish(h):
        y_copy(h, 3).wait_recv()
        flow = acc[h, 3] + yrecv[h, 3].astype(F32)
        for j in range(3):
            z_arrival(h, j).wait_recv()
            flow = flow + zrecv[h, j].astype(F32)
        flow_t[h] = flow
        limit = pred_t[2]
        grad = ((flow - pred_t[h]) + jax.nn.sigmoid(4.0 * (flow - limit))
                - jax.nn.sigmoid(4.0 * (-flow - limit)))
        ag[h, 3] = grad.astype(BF16)
        for i in range(3):
            az_copy(h, i).start()
        ay_copy(h, 3).start()
        ac_copy(h, 3).start()

    def pass_z(h):
        for i in range(3):
            az_arrival(h, i).wait_recv()
            ay_copy(h, i).start()
            ac_copy(h, i).start()

    def pass_y(h):
        for i in (3, 0, 1, 2):
            ay_copy(h, i).wait_recv()
            ac_copy(h, 4 + i).start()

    def backward(h, group):
        g = ag[h, pl.ds(group * 4, 4)].reshape(768, 128)
        return jnp.dot(dense_t[group], g, preferred_element_type=F32)

    def add_own(h):
        total[h] = backward(h, 0) + backward(h, 1)

    def add_core(h):
        for i in (3, 0, 1, 2):
            ac_copy(h, i).wait_recv()
        total[h] += backward(h, 2)
        for i in (7, 4, 5, 6):
            ac_copy(h, i).wait_recv()
        total[h] += backward(h, 3)

    finish(0)
    fx_copy = copy(flow_t.at[0], fx_recv, fx_sem.at[0], fx_sem.at[1], x_mate)
    fx_copy.start()
    finish(1)
    pass_z(0)
    pass_y(0)
    pass_z(1)
    add_own(0)
    add_core(0)
    gx_copy = copy(total.at[0], gx_recv, gx_sem.at[0], gx_sem.at[1], x_mate)
    gx_copy.start()
    pass_y(1)
    add_own(1)
    add_core(1)
    gx_copy.wait_recv()
    gsend[...] = (total[1] + gx_recv[...]).T.reshape(16, 8, 256).astype(BF16)

    def out_copy(k):
        d = (b + k) % 16
        src = (b + 16 - k) % 16
        out = copy(gsend.at[d], grecv.at[b], out_ss.at[k], out_rs.at[k], (s, d))
        inn = copy(gsend.at[d], grecv.at[src], out_ss.at[k], out_rs.at[k], (s, d))
        return out, inn

    def out_start(k, carry):
        out_copy(k)[0].start()
        return carry

    lax.fori_loop(1, 16, out_start, 0)
    grecv[b] = gsend[b]

    fx_copy.wait_recv()
    for m in range(3):
        rows_m = pl.ds(m * 64, 64)
        mine_m, other_m = flow_t[1, rows_m, :], fx_recv[rows_m, :]
        top = jnp.where(first, mine_m, other_m)
        low = jnp.where(first, other_m, mine_m)
        fout_ref[:, pl.ds(m * 128, 128)] = jnp.concatenate([top, low], axis=0).T

    def sent_inj(k, carry):
        inj_copy(k)[0].wait_send()
        return carry

    lax.fori_loop(1, 32, sent_inj, 0)

    for h in range(2):
        def sent_c(k, carry):
            c_copy(h, k).wait_send()
            ac_copy(h, k).wait_send()
            return carry

        lax.fori_loop(0, 8, sent_c, 0)

        def sent_y(k, carry):
            y_copy(h, k).wait_send()
            ay_copy(h, k).wait_send()
            return carry

        lax.fori_loop(0, 4, sent_y, 0)
        for i in range(3):
            z_copy(h, i).wait_send()
            az_copy(h, i).wait_send()
    pred_copy.wait_send()
    fx_copy.wait_send()
    gx_copy.wait_send()

    def out_wait(k, carry):
        out_copy(k)[1].wait_recv()
        return carry

    lax.fori_loop(1, 16, out_wait, 0)
    for k in range(16):
        gout_ref[:, pl.ds(k * 256, 256)] = grecv[k]

    def sent_out(k, carry):
        out_copy(k)[0].wait_send()
        return carry

    lax.fori_loop(1, 16, sent_out, 0)


def store_both(grad_src, flow_src, grad_dst, flow_dst, sems):
    copies = [pltpu.make_async_copy(grad_src, grad_dst, sems.at[0]),
              pltpu.make_async_copy(flow_src, flow_dst, sems.at[1])]
    for item in copies:
        item.start()
    for item in copies:
        item.wait()


def fused(injections, tile_values, tile_line, tile_bus, flow_pred, line_limit):
    vmem = pl.BlockSpec(memory_space=pltpu.VMEM)
    dma = pltpu.SemaphoreType.DMA
    block, half = (192, 256), (192, 128)
    shapes = (jax.ShapeDtypeStruct((8, 4096), BF16), jax.ShapeDtypeStruct((128, 384), F32))
    results = pl.pallas_call(
        kernel,
        out_shape=shapes,
        in_specs=[pl.BlockSpec(memory_space=pl.ANY)] * 6,
        out_specs=(vmem, vmem),
        scratch_shapes=[
            pltpu.VMEM((8, 4096), BF16),
            pltpu.VMEM((64, 64, 128), BF16),
            pltpu.VMEM((1, 64), jnp.int32),
            pltpu.VMEM((1, 64), jnp.int32),
            pltpu.VMEM((128, 384), BF16),
            pltpu.VMEM((384,), jnp.int32),
            pltpu.VMEM((8, 128), jnp.int32),
            pltpu.SMEM((8, 128), jnp.int32),
            pltpu.VMEM((32, 8, 256), BF16),
            pltpu.VMEM((256, 256), BF16),
            pltpu.VMEM((16,) + block, BF16),
            pltpu.VMEM((4, 256, 768), BF16),
            pltpu.VMEM((2, 8) + half, BF16),
            pltpu.VMEM((2, 8) + half, BF16),
            pltpu.VMEM((2, 4) + half, BF16),
            pltpu.VMEM((2, 4) + half, BF16),
            pltpu.VMEM((4,) + half, F32),
            pltpu.VMEM((2, 4) + half, F32),
            pltpu.VMEM((2, 3) + half, BF16),
            pltpu.VMEM((2, 3) + half, BF16),
            pltpu.VMEM((128, 384), BF16),
            pltpu.VMEM((3,) + half, F32),
            pltpu.VMEM((2,) + half, F32),
            pltpu.VMEM(half, F32),
            pltpu.VMEM((2, 16) + half, BF16),
            pltpu.VMEM((2, 256, 128), F32),
            pltpu.VMEM((256, 128), F32),
            pltpu.VMEM((16, 8, 256), BF16),
            pltpu.VMEM((16, 8, 256), BF16),
            dma((6,)), dma, dma((32,)), dma((32,)), dma((2,)),
            dma((2, 8)), dma((2, 8)), dma((2, 4)), dma((2, 4)), dma((2, 3)), dma((2, 3)),
            dma((2,)), dma((2, 3)), dma((2, 3)), dma((2, 4)), dma((2, 4)), dma((2, 8)), dma((2, 8)),
            dma((2,)), dma((16,)), dma((16,)),
        ],
        compiler_params=pltpu.CompilerParams(
            collective_id=0, has_side_effects=True, vmem_limit_bytes=56 * 1024 * 1024),
    )(injections, tile_values, tile_line.reshape(1, -1), tile_bus.reshape(1, -1), flow_pred,
      line_limit)
    anywhere = pl.BlockSpec(memory_space=pl.ANY)
    return pl.pallas_call(
        store_both, out_shape=shapes, in_specs=[anywhere] * 2, out_specs=(anywhere, anywhere),
        scratch_shapes=[dma((2,))],
        compiler_params=pltpu.CompilerParams(vmem_limit_bytes=56 * 1024 * 1024),
    )(*results)


def per_device(injections, tile_values, tile_line, tile_bus, flow_pred, line_limit):
    bus_count = lax.axis_size("bus")
    local_inj = lax.all_to_all(injections, "bus", split_axis=1, concat_axis=0, tiled=True)
    tile_full = lax.all_gather(tile_values, "scen", axis=1, tiled=True)
    tile_count = tile_full.shape[0]
    tile_size = tile_full.shape[1]
    row_count = local_inj.shape[0]
    blocks_here = local_inj.shape[1] // tile_size
    line_blocks = flow_pred.shape[1] // tile_size
    per_owner = tile_count // bus_count
    capacity = per_owner + max(1, tile_count // (2 * bus_count))
    slot_total = bus_count * capacity
    inj_blocks = local_inj.reshape(row_count, blocks_here, tile_size)
    per_tile_inj = jnp.take(inj_blocks, tile_bus, axis=1)
    partial_flows = jnp.einsum(
        "stb,tlb->tsl", per_tile_inj, tile_full, preferred_element_type=jnp.float32
    )
    owner_index = tile_line // line_blocks
    within_owner = tile_line % line_blocks
    owner_hits = (owner_index[:, None] == jnp.arange(bus_count, dtype=jnp.int32)[None, :]).astype(
        jnp.int32
    )
    rank_within = jnp.sum(jnp.cumsum(owner_hits, axis=0) * owner_hits, axis=1) - 1
    slot_index = owner_index * capacity + rank_within
    send_buffer = (
        jnp.zeros((slot_total, row_count, tile_size), jnp.float32).at[slot_index].set(partial_flows)
    )
    slot_label = jnp.full((slot_total,), -1, jnp.int32).at[slot_index].set(within_owner)
    received, received_label = (
        lax.all_to_all(send_buffer, "bus", split_axis=0, concat_axis=0, tiled=True),
        lax.all_to_all(slot_label, "bus", split_axis=0, concat_axis=0, tiled=True),
    )
    select_mask = (
        received_label[None, :] == jnp.arange(line_blocks, dtype=jnp.int32)[:, None]
    ).astype(jnp.float32)
    flow_blocks = jnp.einsum("ms,srl->rml", select_mask, received, precision=lax.Precision.HIGHEST)
    flows = flow_blocks.reshape(row_count, line_blocks * tile_size)
    line_cap = line_limit.astype(jnp.float32) * 0.01
    residual = flows - flow_pred.astype(jnp.float32)
    grad_flow = (
        residual
        + jax.nn.sigmoid(4.0 * (flows - line_cap))
        - jax.nn.sigmoid(4.0 * (-flows - line_cap))
    ).astype(jnp.bfloat16)
    gathered = lax.all_gather(grad_flow, "bus", axis=1, tiled=True)
    gathered_blocks = gathered.reshape(row_count, gathered.shape[1] // tile_size, tile_size)
    per_tile_grad = jnp.take(gathered_blocks, tile_line, axis=1)
    contrib = jnp.einsum(
        "stl,tlb->stb", per_tile_grad, tile_full, preferred_element_type=jnp.float32
    )
    bus_select = (tile_bus[:, None] == jnp.arange(blocks_here, dtype=jnp.int32)[None, :]).astype(
        jnp.float32
    )
    grad_blocks_bus = jnp.einsum(
        "stb,tk->skb", contrib, bus_select, precision=lax.Precision.HIGHEST
    )
    grad_local = grad_blocks_bus.reshape(row_count, blocks_here * tile_size).astype(jnp.bfloat16)
    grad_injections = lax.all_to_all(grad_local, "bus", split_axis=0, concat_axis=1, tiled=True)
    return (grad_injections, flows)


def solution(mesh):
    small = mesh.shape["scen"] == 2 and mesh.shape["bus"] == 16
    return jax.shard_map(
        fused if small else per_device,
        mesh=mesh,
        in_specs=(
            P(("scen", "bus"), None),
            P("bus", "scen", None),
            P("bus"),
            P("bus"),
            P("scen", "bus"),
            P("bus"),
        ),
        out_specs=(P(("scen", "bus"), None), P("scen", "bus")),
        check_vma=False,
    )
```

```python
import jax
import jax.numpy as jnp
from jax import lax
from jax.experimental import pallas as pl
from jax.experimental.pallas import tpu as pltpu
from jax.sharding import PartitionSpec as P

MESH_ID = pl.DeviceIdType.MESH
F32 = jnp.float32
BF16 = jnp.bfloat16


def kernel(inj_hbm, tiles_hbm, line_hbm, busid_hbm, pred_hbm, lim_hbm, gout_ref, fout_ref,
           inj_ref, tiles_ref, line_ref, busid_ref, pred_ref, lim_ref,
           table_v, table_s, inj_buf, inj_t, dense, dense_t,
           csend, crecv, ysend, yrecv, stash, acc, zsend, zrecv,
           pred_recv, pred_t, flow_t, fx_recv,
           ag, total, gx_recv, gsend, grecv,
           in_sem, table_sem, inj_ss, inj_rs, pred_sem, c_ss, c_rs, y_ss, y_rs, z_ss, z_rs,
           fx_sem, az_ss, az_rs, ay_ss, ay_rs, ac_ss, ac_rs, gx_sem, out_ss, out_rs):
    s = lax.axis_index("scen")
    b = lax.axis_index("bus")
    c = b % 2
    y = (b // 2) % 2
    z = b // 4
    me = s * 16 + b
    core_mate = (s, b + 1 - 2 * c)
    y_mate = (s, b + 2 - 4 * y)
    x_mate = (1 - s, b)
    first = s == 0

    loads = [pltpu.make_async_copy(src, dst, in_sem.at[n]) for n, (src, dst) in enumerate((
        (line_hbm, line_ref), (busid_hbm, busid_ref), (tiles_hbm, tiles_ref),
        (inj_hbm, inj_ref), (pred_hbm, pred_ref), (lim_hbm, lim_ref)))]
    for load in loads:
        load.start()

    def zdev(i):
        return (s, ((z + 1 + i) % 4) * 4 + y * 2 + c)

    def copy(src, dst, ss, rs, dev):
        return pltpu.make_async_remote_copy(
            src_ref=src, dst_ref=dst, send_sem=ss, recv_sem=rs,
            device_id=dev, device_id_type=MESH_ID)

    barrier = pltpu.get_barrier_semaphore()

    def greet(k, carry):
        d = (me + k) % 32
        pl.semaphore_signal(barrier, inc=1, device_id=(d // 16, d % 16), device_id_type=MESH_ID)
        return carry

    lax.fori_loop(1, 32, greet, 0)

    loads[0].wait()
    loads[1].wait()
    row = line_ref[...]
    sub = lax.broadcasted_iota(jnp.int32, (64, 64), 0)
    lane = lax.broadcasted_iota(jnp.int32, (64, 64), 1)
    rows = jnp.broadcast_to(row, (64, 64))
    diag = sub == lane
    col = jnp.sum(jnp.where(diag, rows, 0), axis=1, keepdims=True)
    bus_col = jnp.sum(jnp.where(diag, jnp.broadcast_to(busid_ref[...], (64, 64)), 0), axis=1, keepdims=True)
    owner_row = rows // 3
    owner_col = col // 3
    same = jnp.where((owner_row == owner_col) & (lane < sub), 1, 0)
    rank = jnp.sum(same, axis=1, keepdims=True)
    place = owner_col * 6 + rank
    tcol = lax.broadcasted_iota(jnp.int32, (64, 1), 0)
    code = tcol * 8 + (col - owner_col * 3 + 1) * 2 + bus_col
    slot_ids = lax.broadcasted_iota(jnp.int32, (64, 128), 1)
    table = jnp.sum(jnp.where(place == slot_ids, code, 0), axis=0, keepdims=True)
    table_v[...] = jnp.broadcast_to(table, (8, 128))
    to_smem = pltpu.make_async_copy(table_v, table_s, table_sem)
    to_smem.start()
    pl.semaphore_wait(barrier, 31)

    def inj_copy(k):
        d = (me + k) % 32
        src = (me + 32 - k) % 32
        db = d % 16
        out = copy(inj_hbm.at[:, pl.ds(pl.multiple_of(db * 256, 256), 256)],
                   inj_buf.at[me], inj_ss.at[k], inj_rs.at[k], (d // 16, db))
        inn = copy(inj_hbm.at[:, pl.ds(pl.multiple_of(db * 256, 256), 256)],
                   inj_buf.at[src], inj_ss.at[k], inj_rs.at[k], (d // 16, db))
        return out, inn

    def inj_start(k, carry):
        inj_copy(k)[0].start()
        return carry

    lax.fori_loop(1, 32, inj_start, 0)
    pred_copy = copy(pred_hbm, pred_recv, pred_sem.at[0], pred_sem.at[1], x_mate)
    pred_copy.start()
    loads[3].wait()
    inj_buf[me] = inj_ref[:, pl.ds(pl.multiple_of(b * 256, 256), 256)]

    to_smem.wait()
    loads[2].wait()

    def build(r, carry):
        zz = (z + 1 + r % 4) % 4
        yy = (y + (r // 4) % 2) % 2
        cc = (c + r // 8) % 2
        o = zz * 4 + yy * 2 + cc
        tiles = []
        for j in range(6):
            v = table_s[0, o * 6 + j]
            tiles.append((tiles_ref[v // 8].astype(F32), (v // 2) % 4, v % 2))
        for m in range(3):
            for bb in range(2):
                part = jnp.zeros((64, 128), F32)
                for tile, blk, bus in tiles:
                    w = jnp.where((blk == m + 1) & (bus == bb), 1.0, 0.0).astype(F32)
                    part = part + tile * w
                dense[r, pl.ds(m * 64, 64), pl.ds(bb * 128, 128)] = part.astype(BF16)
        return carry

    lax.fori_loop(0, 16, build, 0)

    def inj_wait(k, carry):
        inj_copy(k)[1].wait_recv()
        return carry

    lax.fori_loop(1, 32, inj_wait, 0)
    turned = inj_buf[...].astype(F32).reshape(256, 256).T.astype(BF16)
    inj_t[...] = jnp.where(first, jnp.concatenate([turned[:, 128:], turned[:, :128]], axis=1), turned)

    def forward(group):
        rows = dense[pl.ds(group * 4, 4)].reshape(768, 256)
        return jnp.dot(rows, inj_t[...], preferred_element_type=F32).reshape(4, 192, 256)

    def c_copy(h, k):
        return copy(csend.at[h, k], crecv.at[h, k], c_ss.at[h, k], c_rs.at[h, k], core_mate)

    def y_copy(h, k):
        return copy(ysend.at[h, k], yrecv.at[h, k], y_ss.at[h, k], y_rs.at[h, k], y_mate)

    def z_copy(h, i):
        return copy(zsend.at[h, i], zrecv.at[h, 2 - i], z_ss.at[h, i], z_rs.at[h, 2 - i], zdev(i))

    def z_arrival(h, j):
        return copy(zsend.at[h, j], zrecv.at[h, j], z_ss.at[h, j], z_rs.at[h, j], zdev(j))

    def send_core(group):
        part = forward(2 + group).astype(BF16)
        for h in range(2):
            for i in range(4):
                csend[h, group * 4 + i] = part[i, :, h * 128:h * 128 + 128]
                c_copy(h, group * 4 + i).start()

    def turn(group):
        dense_t[group] = dense[pl.ds(group * 4, 4)].reshape(768, 256).T

    def send_z(h, i):
        y_copy(h, i).wait_recv()
        zsend[h, i] = (acc[h, i] + yrecv[h, i].astype(F32)).astype(BF16)
        z_copy(h, i).start()

    send_core(1)
    far = forward(1)
    for i in range(4):
        stash[i] = far[i, :, 128:]
        c_copy(0, 4 + i).wait_recv()
        ysend[0, i] = (far[i, :, :128] + crecv[0, 4 + i].astype(F32)).astype(BF16)
        y_copy(0, i).start()
    send_core(0)
    for i in range(4):
        c_copy(1, 4 + i).wait_recv()
        ysend[1, i] = (stash[i] + crecv[1, 4 + i].astype(F32)).astype(BF16)
        y_copy(1, i).start()
    near = forward(0)
    for h in range(2):
        for i in range(4):
            c_copy(h, i).wait_recv()
            acc[h, i] = near[i, :, h * 128:h * 128 + 128] + crecv[h, i].astype(F32)
    for i in range(3):
        send_z(0, i)
        turn(i)
    loads[4].wait()
    loads[5].wait()
    pred_copy.wait_recv()
    mine = pred_ref[...].astype(F32).T
    theirs = pred_recv[...].astype(F32).T
    lim_all = jnp.broadcast_to(lim_ref[...].astype(F32)[None, :] * 0.01, (128, 384)).T
    for m in range(3):
        upper, lower = slice(m * 128, m * 128 + 64), slice(m * 128 + 64, m * 128 + 128)
        for n, array in enumerate((theirs, mine, lim_all)):
            pred_t[n, pl.ds(m * 64, 64), :] = jnp.where(first, array[upper], array[lower])
    for i in range(3):
        send_z(1, i)
    turn(3)

    def az_copy(h, i):
        return copy(ag.at[h, 3], ag.at[h, 2 - i], az_ss.at[h, i], az_rs.at[h, 2 - i], zdev(i))

    def az_arrival(h, j):
        return copy(ag.at[h, 3], ag.at[h, j], az_ss.at[h, j], az_rs.at[h, j], zdev(j))

    def ay_copy(h, i):
        return copy(ag.at[h, i], ag.at[h, 4 + i], ay_ss.at[h, i], ay_rs.at[h, i], y_mate)

    def ac_copy(h, i):
        return copy(ag.at[h, i], ag.at[h, 8 + i], ac_ss.at[h, i], ac_rs.at[h, i], core_mate)

    def finish(h):
        y_copy(h, 3).wait_recv()
        flow = acc[h, 3] + yrecv[h, 3].astype(F32)
        for j in range(3):
            z_arrival(h, j).wait_recv()
            flow = flow + zrecv[h, j].astype(F32)
        flow_t[h] = flow
        limit = pred_t[2]
        grad = ((flow - pred_t[h]) + jax.nn.sigmoid(4.0 * (flow - limit))
                - jax.nn.sigmoid(4.0 * (-flow - limit)))
        ag[h, 3] = grad.astype(BF16)
        for i in range(3):
            az_copy(h, i).start()
        ay_copy(h, 3).start()
        ac_copy(h, 3).start()

    def pass_z(h):
        for i in range(3):
            az_arrival(h, i).wait_recv()
            ay_copy(h, i).start()
            ac_copy(h, i).start()

    def pass_y(h):
        for i in (3, 0, 1, 2):
            ay_copy(h, i).wait_recv()
            ac_copy(h, 4 + i).start()

    def backward(h, group):
        g = ag[h, pl.ds(group * 4, 4)].reshape(768, 128)
        return jnp.dot(dense_t[group], g, preferred_element_type=F32)

    def add_own(h):
        total[h] = backward(h, 0) + backward(h, 1)

    def add_core(h):
        for i in (3, 0, 1, 2):
            ac_copy(h, i).wait_recv()
        total[h] += backward(h, 2)
        for i in (7, 4, 5, 6):
            ac_copy(h, i).wait_recv()
        total[h] += backward(h, 3)

    finish(0)
    fx_copy = copy(flow_t.at[0], fx_recv, fx_sem.at[0], fx_sem.at[1], x_mate)
    fx_copy.start()
    finish(1)
    pass_z(0)
    pass_y(0)
    pass_z(1)
    add_own(0)
    add_core(0)
    gx_copy = copy(total.at[0], gx_recv, gx_sem.at[0], gx_sem.at[1], x_mate)
    gx_copy.start()
    pass_y(1)
    add_own(1)
    add_core(1)
    gx_copy.wait_recv()
    gsend[...] = (total[1] + gx_recv[...]).T.reshape(16, 8, 256).astype(BF16)

    def out_copy(k):
        d = (b + k) % 16
        src = (b + 16 - k) % 16
        out = copy(gsend.at[d], grecv.at[b], out_ss.at[k], out_rs.at[k], (s, d))
        inn = copy(gsend.at[d], grecv.at[src], out_ss.at[k], out_rs.at[k], (s, d))
        return out, inn

    def out_start(k, carry):
        out_copy(k)[0].start()
        return carry

    lax.fori_loop(1, 16, out_start, 0)
    grecv[b] = gsend[b]

    fx_copy.wait_recv()
    for m in range(3):
        rows_m = pl.ds(m * 64, 64)
        mine_m, other_m = flow_t[1, rows_m, :], fx_recv[rows_m, :]
        top = jnp.where(first, mine_m, other_m)
        low = jnp.where(first, other_m, mine_m)
        fout_ref[:, pl.ds(m * 128, 128)] = jnp.concatenate([top, low], axis=0).T

    def sent_inj(k, carry):
        inj_copy(k)[0].wait_send()
        return carry

    lax.fori_loop(1, 32, sent_inj, 0)

    for h in range(2):
        def sent_c(k, carry):
            c_copy(h, k).wait_send()
            ac_copy(h, k).wait_send()
            return carry

        lax.fori_loop(0, 8, sent_c, 0)

        def sent_y(k, carry):
            y_copy(h, k).wait_send()
            ay_copy(h, k).wait_send()
            return carry

        lax.fori_loop(0, 4, sent_y, 0)
        for i in range(3):
            z_copy(h, i).wait_send()
            az_copy(h, i).wait_send()
    pred_copy.wait_send()
    fx_copy.wait_send()
    gx_copy.wait_send()

    def out_wait(k, carry):
        out_copy(k)[1].wait_recv()
        return carry

    lax.fori_loop(1, 16, out_wait, 0)
    for k in range(16):
        gout_ref[:, pl.ds(k * 256, 256)] = grecv[k]

    def sent_out(k, carry):
        out_copy(k)[0].wait_send()
        return carry

    lax.fori_loop(1, 16, sent_out, 0)


def fused(injections, tile_values, tile_line, tile_bus, flow_pred, line_limit):
    vmem = pl.BlockSpec(memory_space=pltpu.VMEM)
    dma = pltpu.SemaphoreType.DMA
    block, half = (192, 256), (192, 128)
    shapes = (jax.ShapeDtypeStruct((8, 4096), BF16), jax.ShapeDtypeStruct((128, 384), F32))
    return pl.pallas_call(
        kernel,
        out_shape=shapes,
        in_specs=[pl.BlockSpec(memory_space=pl.ANY)] * 6,
        out_specs=(vmem, vmem),
        scratch_shapes=[
            pltpu.VMEM((8, 4096), BF16),
            pltpu.VMEM((64, 64, 128), BF16),
            pltpu.VMEM((1, 64), jnp.int32),
            pltpu.VMEM((1, 64), jnp.int32),
            pltpu.VMEM((128, 384), BF16),
            pltpu.VMEM((384,), jnp.int32),
            pltpu.VMEM((8, 128), jnp.int32),
            pltpu.SMEM((8, 128), jnp.int32),
            pltpu.VMEM((32, 8, 256), BF16),
            pltpu.VMEM((256, 256), BF16),
            pltpu.VMEM((16,) + block, BF16),
            pltpu.VMEM((4, 256, 768), BF16),
            pltpu.VMEM((2, 8) + half, BF16),
            pltpu.VMEM((2, 8) + half, BF16),
            pltpu.VMEM((2, 4) + half, BF16),
            pltpu.VMEM((2, 4) + half, BF16),
            pltpu.VMEM((4,) + half, F32),
            pltpu.VMEM((2, 4) + half, F32),
            pltpu.VMEM((2, 3) + half, BF16),
            pltpu.VMEM((2, 3) + half, BF16),
            pltpu.VMEM((128, 384), BF16),
            pltpu.VMEM((3,) + half, F32),
            pltpu.VMEM((2,) + half, F32),
            pltpu.VMEM(half, F32),
            pltpu.VMEM((2, 16) + half, BF16),
            pltpu.VMEM((2, 256, 128), F32),
            pltpu.VMEM((256, 128), F32),
            pltpu.VMEM((16, 8, 256), BF16),
            pltpu.VMEM((16, 8, 256), BF16),
            dma((6,)), dma, dma((32,)), dma((32,)), dma((2,)),
            dma((2, 8)), dma((2, 8)), dma((2, 4)), dma((2, 4)), dma((2, 3)), dma((2, 3)),
            dma((2,)), dma((2, 3)), dma((2, 3)), dma((2, 4)), dma((2, 4)), dma((2, 8)), dma((2, 8)),
            dma((2,)), dma((16,)), dma((16,)),
        ],
        compiler_params=pltpu.CompilerParams(
            collective_id=0, has_side_effects=True, vmem_limit_bytes=56 * 1024 * 1024),
    )(injections, tile_values, tile_line.reshape(1, -1), tile_bus.reshape(1, -1), flow_pred,
      line_limit)


def per_device(injections, tile_values, tile_line, tile_bus, flow_pred, line_limit):
    bus_count = lax.axis_size("bus")
    local_inj = lax.all_to_all(injections, "bus", split_axis=1, concat_axis=0, tiled=True)
    tile_full = lax.all_gather(tile_values, "scen", axis=1, tiled=True)
    tile_count = tile_full.shape[0]
    tile_size = tile_full.shape[1]
    row_count = local_inj.shape[0]
    blocks_here = local_inj.shape[1] // tile_size
    line_blocks = flow_pred.shape[1] // tile_size
    per_owner = tile_count // bus_count
    capacity = per_owner + max(1, tile_count // (2 * bus_count))
    slot_total = bus_count * capacity
    inj_blocks = local_inj.reshape(row_count, blocks_here, tile_size)
    per_tile_inj = jnp.take(inj_blocks, tile_bus, axis=1)
    partial_flows = jnp.einsum(
        "stb,tlb->tsl", per_tile_inj, tile_full, preferred_element_type=jnp.float32
    )
    owner_index = tile_line // line_blocks
    within_owner = tile_line % line_blocks
    owner_hits = (owner_index[:, None] == jnp.arange(bus_count, dtype=jnp.int32)[None, :]).astype(
        jnp.int32
    )
    rank_within = jnp.sum(jnp.cumsum(owner_hits, axis=0) * owner_hits, axis=1) - 1
    slot_index = owner_index * capacity + rank_within
    send_buffer = (
        jnp.zeros((slot_total, row_count, tile_size), jnp.float32).at[slot_index].set(partial_flows)
    )
    slot_label = jnp.full((slot_total,), -1, jnp.int32).at[slot_index].set(within_owner)
    received, received_label = (
        lax.all_to_all(send_buffer, "bus", split_axis=0, concat_axis=0, tiled=True),
        lax.all_to_all(slot_label, "bus", split_axis=0, concat_axis=0, tiled=True),
    )
    select_mask = (
        received_label[None, :] == jnp.arange(line_blocks, dtype=jnp.int32)[:, None]
    ).astype(jnp.float32)
    flow_blocks = jnp.einsum("ms,srl->rml", select_mask, received, precision=lax.Precision.HIGHEST)
    flows = flow_blocks.reshape(row_count, line_blocks * tile_size)
    line_cap = line_limit.astype(jnp.float32) * 0.01
    residual = flows - flow_pred.astype(jnp.float32)
    grad_flow = (
        residual
        + jax.nn.sigmoid(4.0 * (flows - line_cap))
        - jax.nn.sigmoid(4.0 * (-flows - line_cap))
    ).astype(jnp.bfloat16)
    gathered = lax.all_gather(grad_flow, "bus", axis=1, tiled=True)
    gathered_blocks = gathered.reshape(row_count, gathered.shape[1] // tile_size, tile_size)
    per_tile_grad = jnp.take(gathered_blocks, tile_line, axis=1)
    contrib = jnp.einsum(
        "stl,tlb->stb", per_tile_grad, tile_full, preferred_element_type=jnp.float32
    )
    bus_select = (tile_bus[:, None] == jnp.arange(blocks_here, dtype=jnp.int32)[None, :]).astype(
        jnp.float32
    )
    grad_blocks_bus = jnp.einsum(
        "stb,tk->skb", contrib, bus_select, precision=lax.Precision.HIGHEST
    )
    grad_local = grad_blocks_bus.reshape(row_count, blocks_here * tile_size).astype(jnp.bfloat16)
    grad_injections = lax.all_to_all(grad_local, "bus", split_axis=0, concat_axis=1, tiled=True)
    return (grad_injections, flows)


def solution(mesh):
    small = mesh.shape["scen"] == 2 and mesh.shape["bus"] == 16
    return jax.shard_map(
        fused if small else per_device,
        mesh=mesh,
        in_specs=(
            P(("scen", "bus"), None),
            P("bus", "scen", None),
            P("bus"),
            P("bus"),
            P("scen", "bus"),
            P("bus"),
        ),
        out_specs=(P(("scen", "bus"), None), P("scen", "bus")),
        check_vma=False,
    )
```
